32 devices in a mesh: groups: 2 (over y), seq: 8 (over z, x), head: 2 (over core).
Axes of the slice: x: 2, y: 2, z: 4, core: 2. Of those that a mesh axis runs over, the one named last changes fastest.
Arguments:
- text_query_rows: bfloat16 [2048, 8192], P(('groups', 'seq'), 'head'), parts along dimension 0, may hold values from -40 to 40, as said below
- text_key_value: bfloat16 [2, 2048, 1024], P(None, ('groups', 'seq'), 'head'), parts along dimension 1, may hold values from -4 to 4, as said below
- doc_ids: int32 [2048], P(('groups', 'seq')), parts along dimension 0, may hold values from 0 to 3, never falling along the last dimension, each value on 1 to 512 neighbouring positions
- tile_span: int32 [2048, 2], P(('groups', 'seq')), parts along dimension 0, may hold values from 0 to 8, as said below
- vision_hidden: bfloat16 [4096, 1280], P(('groups', 'seq')), parts along dimension 0, may hold values from -6 to 6
- vision_qkv: bfloat16 [3, 4096, 1280], P(None, ('groups', 'seq'), 'head'), parts along dimension 1, may hold values from -6 to 6, as said below
- vision_out_weight: bfloat16 [1280, 1280], P('head'), may hold values from -0.625 to 0.625
- cross_keyvalue_weight: bfloat16 [1280, 2, 1024], P('seq', None, 'head'), may hold values from -0.15625 to 0.15625
- cross_gate: float32 [64], P('head'), may hold values from -1.5 to 1.5
Outputs:
- attention_out: bfloat16 [2048, 8192], P(('groups', 'seq'), 'head'), parts along dimension 0
The draws below stay inside these ranges and needn't reach their ends.
There are 2 independent parts, one for each index of `groups`. The reference program is written for one: setup_inputs(seed, part) draws one part's arguments, and reference() takes and returns one part's arrays. A program takes and returns all parts, laid end to end along the dimension named above; an argument that names none is the same for every part. Nothing has to cross between parts.
Inputs may be any that keep to these rules, and one draw needn't show every extreme that they name: `tile_span`: each text token's span is an interval of the tiles of its own block b = p // 128 and of block b - 1 (first <= second, both between b - 1 and b + 1, never below 0); it may be empty. `doc_ids`: never falling along the document; each segment holds 1 to 512 tokens. `text_query_rows`: real values. `text_key_value`: real values. `vision_qkv`: real values.
All inputs are finite; a program needn't handle non-finite values.
Results may differ from the reference program's by a relative error of at most 0.024.
Values may be sent and summed in bfloat16 or wider, within the bound.
A program may use at most 64 MiB of HBM per device.

```python
import math
import jax
import jax.numpy as jnp
import numpy as np
from jax import lax

QUERY_HEADS = 64
KEY_VALUE_HEADS = 8
HEAD_SIZE = 128
VISION_LAYER_WIDTH = 1280
VH = 16
VHD = 80
BLOCK_TOKENS = 128
TILE_WINDOW_ROWS = 256
WINDOW_BLOCKS = 2
DOCUMENT_TOKENS = 1024
IMG_TOK = 2048
DOCS = 4
N_SEQ = 8


def text_pair(key):
    key_value_random = jax.random.fold_in(key, 7)
    query_key = jax.random.fold_in(key, 8)
    key_value = jnp.clip(jax.random.normal(key_value_random, (2, DOCUMENT_TOKENS, KEY_VALUE_HEADS * HEAD_SIZE), jnp.float32), -4.0, 4.0)
    query_rows = jnp.clip(jax.random.normal(query_key, (DOCUMENT_TOKENS, QUERY_HEADS * HEAD_SIZE), jnp.float32), -4.0, 4.0)
    return (query_rows, key_value)


def draw_text_query_rows(key, part):
    return text_pair(key)[0].astype(jnp.bfloat16)


def draw_text_key_value(key, part):
    return text_pair(key)[1].astype(jnp.bfloat16)


def draw_vision_qkv(key, part):
    result = jnp.clip(jax.random.normal(jax.random.fold_in(key, 21), (3, IMG_TOK, VISION_LAYER_WIDTH), jnp.float32), -6.0, 6.0)
    return result.astype(jnp.bfloat16)


def draw_tile_span(key, part):
    positions = jnp.arange(DOCUMENT_TOKENS, dtype=jnp.int32)
    block_ids = positions // BLOCK_TOKENS
    modes = jax.random.randint(jax.random.fold_in(key, 3), (DOCUMENT_TOKENS,), 0, 4)
    low_tile = jnp.where((modes == 1) | (modes == 3), block_ids - 1, block_ids)
    high_tile = jnp.where((modes == 1) | (modes == 0), block_ids, block_ids + 1)
    low_tile = jnp.maximum(low_tile, 0)
    high_tile = jnp.maximum(high_tile, low_tile)
    return jnp.stack([low_tile, high_tile], axis=1).astype(jnp.int32)


def shard_levels(own_key, dims, shards, low, largest):
    loudness, own = 1.0, jax.random.fold_in(own_key, 6)
    for dim, blocks in shards:
        steps = jnp.exp(jax.random.uniform(jax.random.fold_in(own, dim), (blocks,), jnp.float32, low / len(shards), largest / len(shards)))
        loudness = loudness * jnp.repeat(steps, dims[dim] // blocks).reshape([-1 if axis == dim else 1 for axis in range(len(dims))])
    return loudness


def split_up(number_of, total, bound, skew):
    weights = [(1 << 20) // math.isqrt(grade ** skew) + 1 for grade in range(2, number_of + 1)]
    spare, counts = total - bound - (number_of - 1), [1] * (number_of - 1)
    while spare > 0:
        movable = [i for i in range(number_of - 1) if counts[i] < bound]
        pool, left = sum([weights[i] for i in movable]), spare
        for i in movable:
            extra = min(bound - counts[i], max(1, left * weights[i] // pool), spare)
            counts[i] = counts[i] + extra
            spare = spare - extra
    return np.array([bound] + counts)


def uneven_parts(rng, number_of, total, limit, lean):
    if number_of == 2:
        one = jax.random.randint(rng, (), max(1, total - limit), min(limit, total - 1) + 1)
        return jnp.stack([one, total - one])
    lengths = jnp.asarray(split_up(number_of, total, limit, lean), jnp.int32)
    pairs = (number_of - 1) // 2
    source_of, taker = lengths[1:1 + 2 * pairs:2], lengths[2:2 + 2 * pairs:2]
    room = jnp.minimum(source_of - 1, limit - taker)
    moved = jax.random.randint(jax.random.fold_in(rng, 1), (pairs,), 0, 1 << 20) % (room + 1)
    lengths = lengths.at[1:1 + 2 * pairs:2].set(source_of - moved).at[2:2 + 2 * pairs:2].set(taker + moved)
    return lengths[jax.random.permutation(jax.random.fold_in(rng, 2), number_of)]


def normal_values(own_key, extent, scale, most, cuts=(), kind=jnp.bfloat16):
    values = jax.random.normal(own_key, extent, jnp.float32) * scale
    if len(cuts) > 0:
        values = shard_levels(own_key, extent, cuts, -0.22, 0.18) * values
    return jnp.clip(values, min=-most, max=most).astype(kind)


def setup_inputs(seed: int = 0, part: int = 0) -> dict:
    arg_keys = jax.random.split(jax.random.key(seed), 10)
    part_keys = jax.random.split(jax.random.fold_in(arg_keys[9], part), 10)
    return {
        "text_query_rows": draw_text_query_rows(jax.random.fold_in(jax.random.fold_in(arg_keys[9], part), 71), part),
        "text_key_value": draw_text_key_value(jax.random.fold_in(jax.random.fold_in(arg_keys[9], part), 71), part),
        "doc_ids": jnp.searchsorted(jnp.cumsum(uneven_parts(part_keys[2], DOCS, DOCUMENT_TOKENS, 4 * BLOCK_TOKENS, 0)), jnp.arange(DOCUMENT_TOKENS), side="right").astype(jnp.int32),
        "tile_span": draw_tile_span(jax.random.fold_in(jax.random.fold_in(arg_keys[9], part), 71), part),
        "vision_hidden": normal_values(part_keys[4], (IMG_TOK, VISION_LAYER_WIDTH), 1.0, 6.0, ((0, 8),)),
        "vision_qkv": draw_vision_qkv(jax.random.fold_in(jax.random.fold_in(arg_keys[9], part), 71), part),
        "vision_out_weight": normal_values(arg_keys[6], (VISION_LAYER_WIDTH, VISION_LAYER_WIDTH), (VISION_LAYER_WIDTH // 16) ** -0.5, 0.625, ((0, 2),)),
        "cross_keyvalue_weight": normal_values(arg_keys[7], (VISION_LAYER_WIDTH, 2, KEY_VALUE_HEADS * HEAD_SIZE), VISION_LAYER_WIDTH ** -0.5, 0.15625, ((0, 8), (2, 2))),
        "cross_gate": jnp.clip(jax.random.uniform(arg_keys[8], (QUERY_HEADS,), jnp.float32, -1.5, 1.5) * shard_levels(arg_keys[8], (QUERY_HEADS,), ((0, 2),), -0.4, 0.0), -1.5, 1.5),
    }


def attend_heads(query_rows, keys, allowed_mask):
    scores = jnp.einsum('tgrd,kgd->grtk', query_rows, keys, preferred_element_type=jnp.float32) / math.sqrt(HEAD_SIZE)
    scores = jnp.where(allowed_mask[None, None], scores, -1e+30)
    return jax.nn.softmax(scores, axis=-1)

def reference(text_query_rows, text_key_value, doc_ids, tile_span, vision_hidden, vision_qkv, vision_out_weight, cross_keyvalue_weight, cross_gate):
    query_group_ratio = QUERY_HEADS // KEY_VALUE_HEADS

    def vision_tile(tile_number):
        tile_rows = lax.dynamic_slice_in_dim(vision_qkv, tile_number * TILE_WINDOW_ROWS, TILE_WINDOW_ROWS, 1).astype(jnp.float32)
        query_rows = tile_rows[0].reshape(TILE_WINDOW_ROWS, VH, VHD)
        keys = tile_rows[1].reshape(TILE_WINDOW_ROWS, VH, VHD)
        values = tile_rows[2].reshape(TILE_WINDOW_ROWS, VH, VHD)
        scores = jnp.einsum('qhd,khd->hqk', query_rows, keys) / math.sqrt(VHD)
        weights = jax.nn.softmax(scores, axis=-1).astype(jnp.bfloat16)
        mixed_heads = jnp.einsum('hqk,khd->qhd', weights.astype(jnp.float32), values)
        return mixed_heads.astype(jnp.bfloat16).reshape(TILE_WINDOW_ROWS, VISION_LAYER_WIDTH)
    vision_attn = lax.map(vision_tile, jnp.arange(N_SEQ, dtype=jnp.int32)).reshape(IMG_TOK, VISION_LAYER_WIDTH)
    vision_mixed = vision_hidden.astype(jnp.float32) + jnp.dot(vision_attn, vision_out_weight, preferred_element_type=jnp.float32)
    image_norm = (vision_mixed * lax.rsqrt(lax.optimization_barrier(jnp.mean(vision_mixed * vision_mixed, axis=-1, keepdims=True)) + 1e-05)).astype(jnp.bfloat16)
    image_key_value = jnp.einsum('ic,cjf->ijf', image_norm.astype(jnp.float32), cross_keyvalue_weight.astype(jnp.float32)).astype(jnp.bfloat16)
    padded_key_value = jnp.concatenate([jnp.zeros((2, WINDOW_BLOCKS * BLOCK_TOKENS, KEY_VALUE_HEADS * HEAD_SIZE), text_key_value.dtype), text_key_value], axis=1)
    pad_docs = jnp.concatenate([jnp.zeros((WINDOW_BLOCKS * BLOCK_TOKENS,), jnp.int32), doc_ids], axis=0)
    padded_image = jnp.concatenate([jnp.zeros((TILE_WINDOW_ROWS, 2, KEY_VALUE_HEADS * HEAD_SIZE), image_key_value.dtype), image_key_value], axis=0)
    gate_cols = jnp.repeat(jnp.tanh(cross_gate), HEAD_SIZE)

    def text_block(block_number):
        starting_row = block_number * BLOCK_TOKENS
        query_rows = lax.dynamic_slice_in_dim(text_query_rows, starting_row, BLOCK_TOKENS, 0).astype(jnp.float32).reshape(BLOCK_TOKENS, KEY_VALUE_HEADS, query_group_ratio, HEAD_SIZE)
        key_value_pairs = lax.dynamic_slice_in_dim(padded_key_value, starting_row, (WINDOW_BLOCKS + 1) * BLOCK_TOKENS, 1).astype(jnp.float32)
        key_docs = lax.dynamic_slice_in_dim(pad_docs, starting_row, (WINDOW_BLOCKS + 1) * BLOCK_TOKENS, 0)
        own_docs = lax.dynamic_slice_in_dim(doc_ids, starting_row, BLOCK_TOKENS, 0)
        key_pos = starting_row - WINDOW_BLOCKS * BLOCK_TOKENS + jnp.arange((WINDOW_BLOCKS + 1) * BLOCK_TOKENS, dtype=jnp.int32)
        query_pos = starting_row + jnp.arange(BLOCK_TOKENS, dtype=jnp.int32)
        allowed_mask = (key_docs[None, :] == own_docs[:, None]) & (key_pos[None, :] <= query_pos[:, None]) & (key_pos[None, :] >= 0)
        self_attention_weights = attend_heads(query_rows, key_value_pairs[0].reshape(-1, KEY_VALUE_HEADS, HEAD_SIZE), allowed_mask).astype(jnp.bfloat16)
        self_output = jnp.einsum('ycmq,qyb->mycb', self_attention_weights.astype(jnp.float32), key_value_pairs[1].reshape(-1, KEY_VALUE_HEADS, HEAD_SIZE)).reshape(BLOCK_TOKENS, QUERY_HEADS * HEAD_SIZE)
        image_token_rows = lax.dynamic_slice_in_dim(padded_image, block_number * TILE_WINDOW_ROWS, 2 * TILE_WINDOW_ROWS, 0).astype(jnp.float32)
        tile_ids = block_number - 1 + jnp.arange(2 * TILE_WINDOW_ROWS, dtype=jnp.int32) // TILE_WINDOW_ROWS
        span_rows = lax.dynamic_slice_in_dim(tile_span, starting_row, BLOCK_TOKENS, 0)
        low_tile = span_rows[:, 0]
        high_tile = span_rows[:, 1]
        visible_mask = (tile_ids[None, :] >= low_tile[:, None]) & (tile_ids[None, :] < high_tile[:, None])
        image_present = (high_tile > low_tile).astype(jnp.float32)
        cross_probabilities = attend_heads(query_rows, image_token_rows[:, 0].reshape(-1, KEY_VALUE_HEADS, HEAD_SIZE), visible_mask) * image_present[None, None, :, None]
        cross_probabilities = cross_probabilities.astype(jnp.bfloat16)
        cross_output = jnp.einsum('ycmq,qyb->mycb', cross_probabilities.astype(jnp.float32), image_token_rows[:, 1].reshape(-1, KEY_VALUE_HEADS, HEAD_SIZE)).reshape(BLOCK_TOKENS, QUERY_HEADS * HEAD_SIZE)
        return (self_output + gate_cols[None, :] * cross_output).astype(jnp.bfloat16)
    outputs = lax.map(text_block, jnp.arange(N_SEQ, dtype=jnp.int32))
    return outputs.reshape(DOCUMENT_TOKENS, QUERY_HEADS * HEAD_SIZE)
```

```python
import functools
import math

import jax
import jax.numpy as jnp
from jax import lax
from jax.experimental import pallas as pl
from jax.experimental.pallas import tpu as pltpu
from jax.sharding import PartitionSpec as P

HEAD_SIZE = 128
VHD = 80
MESH = pl.DeviceIdType.MESH
BIG = -1e30
LOG2E = math.log2(math.e)
RING_PLACES = 8
F32 = jnp.float32
BF16 = jnp.bfloat16


def dot_t(a, b):
    return lax.dot_general(a, b, (((1,), (1,)), ((), ())), preferred_element_type=F32)


def attend(q, k, v, bias):
    s = dot_t(q, k) * (LOG2E / math.sqrt(HEAD_SIZE)) + bias
    m = jnp.max(s, axis=-1, keepdims=True)
    p = jnp.exp2(s - m).astype(BF16)
    o = jnp.dot(p, jnp.concatenate([v, jnp.ones_like(v)], axis=1), preferred_element_type=F32)
    return o[:, :HEAD_SIZE] / o[:, HEAD_SIZE:]


def kernel(
    n, ring, q_hbm, tkv_hbm, doc_row, doc_col, span, hid_hbm, vqkv_hbm, wo_hbm, w_hbm, gate,
    out,
    q, tkv, docs, hid, vqkv, wo, w, va, mix, img, ikv, self_out, sems, rsems, lsems,
):
    g, s, h = lax.axis_index("groups"), lax.axis_index("seq"), lax.axis_index("head")
    rows = q.shape[0]
    tile = hid.shape[0]
    half = tile // 2
    width = hid.shape[1]
    kv_cols = tkv.shape[2]
    kv_heads = kv_cols // HEAD_SIZE
    ratio = q.shape[1] // kv_cols
    shard = w_hbm.shape[0]
    part = vqkv.shape[2]
    counter = iter(range(64))

    local = []

    def fetch(src, dst):
        c = pltpu.make_async_copy(src, dst, lsems.at[len(local)])
        c.start()
        local.append(c)
        return c

    def remote(src, dst, to):
        i = next(counter)
        return pltpu.make_async_remote_copy(
            src_ref=src, dst_ref=dst, send_sem=sems.at[i], recv_sem=rsems.at[i],
            device_id=to, device_id_type=MESH,
        )

    get_vqkv = fetch(vqkv_hbm, vqkv)
    get_wo = fetch(wo_hbm, wo.at[h])
    get_hid = fetch(hid_hbm, hid)
    my_rows = pl.ds(pl.multiple_of(s * shard, 16), shard) if ring else pl.ds(0, shard)
    get_w = fetch(w_hbm, w.at[my_rows])
    get_tkv = fetch(tkv_hbm, tkv.at[:, pl.ds(2 * rows, rows)])
    get_q = fetch(q_hbm, q)

    sibling = (g, s, 1 - h)
    barrier = pltpu.get_barrier_semaphore()

    def greet(to):
        pl.semaphore_signal(barrier, inc=1, device_id=to, device_id_type=MESH)

    greet(sibling)
    greets = 1
    if ring:
        place = jnp.where(s % 2 == 0, s // 2, RING_PLACES - 1 - s // 2)

        def at_place(r):
            r = (r + RING_PLACES) % RING_PLACES
            return jnp.where(r < RING_PLACES // 2, 2 * r, 2 * RING_PLACES - 1 - 2 * r)

        right, left = (g, at_place(place + 1), h), (g, at_place(place - 1), h)
        partner = (1 - g, s, h)
        for to in (right, left, partner):
            greet(to)
        greets = 4
    for d in (1, 2):
        @pl.when(s + d < n)
        def _():
            greet((g, jnp.minimum(s + d, n - 1), h))

        @pl.when(s - d >= 0)
        def _():
            greet((g, jnp.maximum(s - d, 0), h))
    near = sum(
        jnp.where(s + d < n, 1, 0) + jnp.where(s - d >= 0, 1, 0) for d in (1, 2)
    )
    pl.semaphore_wait(barrier, greets + near)

    if ring:
        over = shard // 16 * 2 // 5 * 16
        share = shard - over
        off = pl.multiple_of(g * over, 16)
        give = pl.multiple_of(g * share, 16)

        def piece(place_of, start, size):
            at = at_place(place_of) * shard + start
            return w.at[pl.ds(pl.multiple_of(at, 16), size)]

        own = w_hbm.at[pl.ds(off, share)]
        cw, ccw, across = [], [], []
        half_share = share // 2

    def ring_start(k):
        if not ring:
            return
        if k < 4:
            a, b = piece(place - k + 1, off, share), piece(place + k - 1, off, share)
            cw.append(remote(own if k == 1 else a, a, right))
            ccw.append(remote(own if k == 1 else b, b, left))
        else:
            a = piece(place - 3, off, half_share)
            b = piece(place + 3, off + half_share, half_share)
            cw.append(remote(a, a, right))
            ccw.append(remote(b, b, left))
        cw[-1].start()
        ccw[-1].start()

    def ring_service(k):
        if not ring:
            return
        cw[k - 1].wait_recv()
        ccw[k - 1].wait_recv()
        if k < 4:
            ring_start(k + 1)
        for at in (place - k, place + k)[: 1 if k == 4 else 2]:
            block = piece(at, give, over)
            across.append(remote(block, block, partner))
            across[-1].start()

    ring_start(1)
    send_wo = remote(wo_hbm, wo.at[h], sibling)
    send_wo.start()
    text = []
    for d in (1, 2):
        to = (g, jnp.minimum(s + d, n - 1), h)
        text.append((
            d,
            remote(tkv_hbm, tkv.at[:, pl.ds((2 - d) * rows, rows)], to),
            remote(doc_row, docs.at[2 - d], to),
        ))

        @pl.when(s + d < n)
        def _():
            text[-1][1].start()
            text[-1][2].start()

        @pl.when(s - d < 0)
        def _():
            tkv[:, (2 - d) * rows : (3 - d) * rows] = jnp.zeros((2, rows, kv_cols), BF16)
            docs[2 - d] = jnp.full((1, rows), -1, jnp.int32)

    @pl.when(s == 0)
    def _():
        img[:tile] = jnp.zeros((tile, width), BF16)

    get_vqkv.wait()
    column = lax.broadcasted_iota(jnp.int32, (tile, 256), 1)
    mix[:, :part] = jnp.zeros((tile, part), F32)
    for head in range(part // VHD):
        start = min(head * VHD // 128 * 128, part - 256)
        first = head * VHD - start
        mine = (column >= first) & (column < first + VHD)
        window = slice(start, start + 256)
        vq = jnp.where(mine, vqkv[0, :, window], jnp.zeros((), BF16))
        sc = dot_t(vq, vqkv[1, :, window]) * (LOG2E / math.sqrt(VHD))
        p = jnp.exp2(sc - jnp.max(sc, axis=-1, keepdims=True))
        p = (p * (1.0 / jnp.sum(p, axis=-1, keepdims=True))).astype(BF16)
        o = jnp.dot(p, vqkv[2, :, window], preferred_element_type=F32)
        mix[:, window] = mix[:, window] + jnp.where(mine, o, 0.0)
        if head == 3:
            ring_service(1)
    va[h] = mix[:, :part].astype(BF16)
    send_va = remote(va.at[h], va.at[h], sibling)
    send_va.start()

    get_wo.wait()
    get_hid.wait()
    mix[...] = hid[...].astype(F32) + jnp.dot(va[h], wo[h], preferred_element_type=F32)
    send_wo.wait_recv()
    send_va.wait_recv()
    mixed = mix[...] + jnp.dot(va[1 - h], wo[1 - h], preferred_element_type=F32)
    norm = mixed * lax.rsqrt(jnp.mean(mixed * mixed, axis=-1, keepdims=True) + 1e-5)
    img[tile:] = norm.astype(BF16)
    mine_prev = img.at[pl.ds(pl.multiple_of(h * half, 16), half)]
    send_img = remote(
        img.at[pl.ds(pl.multiple_of(tile + h * half, 16), half)], mine_prev,
        (g, jnp.minimum(s + 1, n - 1), h),
    )
    pass_img = remote(mine_prev, mine_prev, sibling)

    @pl.when(s + 1 < n)
    def _():
        send_img.start()

    ring_service(2)

    for d, kv_copy, doc_copy in text:
        @pl.when(s - d >= 0)
        def _():
            kv_copy.wait_recv()
            doc_copy.wait_recv()
    get_tkv.wait()
    get_q.wait()
    key_docs = jnp.concatenate([docs[0], docs[1], doc_row[...]], axis=1)
    key_at = lax.broadcasted_iota(jnp.int32, (rows, 3 * rows), 1) - 2 * rows
    query_at = lax.broadcasted_iota(jnp.int32, (rows, 3 * rows), 0)
    seen = (key_docs == doc_col[...]) & (key_at <= query_at) & (key_at + s * rows >= 0)
    bias = jnp.where(seen, 0.0, BIG)
    bias = jnp.concatenate([bias, bias], axis=0)

    def query_pair(kv_head, pair):
        at = pl.multiple_of((kv_head * ratio + 2 * pair) * HEAD_SIZE, 128)
        return at, jnp.concatenate(
            [q[:, pl.ds(at, HEAD_SIZE)], q[:, pl.ds(at + HEAD_SIZE, HEAD_SIZE)]], axis=0
        )

    def self_head(kv_head, _):
        cols = pl.ds(pl.multiple_of(kv_head * HEAD_SIZE, 128), HEAD_SIZE)
        k, v = tkv[0, :, cols], tkv[1, :, cols]
        for pair in range(ratio // 2):
            at, two = query_pair(kv_head, pair)
            o = attend(two, k, v, bias)
            self_out[:, pl.ds(at, HEAD_SIZE)] = o[:rows]
            self_out[:, pl.ds(at + HEAD_SIZE, HEAD_SIZE)] = o[rows:]
        return 0

    lax.fori_loop(0, kv_heads // 2, self_head, 0)
    ring_service(3)

    @pl.when(s >= 1)
    def _():
        send_img.wait_recv()
        pass_img.start()

    lax.fori_loop(kv_heads // 2, kv_heads, self_head, 0)
    ring_service(4)

    @pl.when(s >= 1)
    def _():
        pass_img.wait_recv()

    get_w.wait()
    if ring:
        for c in across:
            c.wait_recv()

    def project(i, _):
        cols = pl.ds(pl.multiple_of(i * 256, 256), 256)
        ikv[:, cols] = jnp.dot(img[...], w[:, cols], preferred_element_type=F32).astype(BF16)
        return 0

    lax.fori_loop(0, ikv.shape[1] // 256, project, 0)

    low, high = span[:, 0:1], span[:, 1:2]
    tile_of = s - 1 + lax.broadcasted_iota(jnp.int32, (rows, 2 * tile), 1) // tile
    seen_tiles = (tile_of >= low) & (tile_of < high)
    tile_bias = jnp.where(seen_tiles, 0.0, BIG)
    tile_bias = jnp.concatenate([tile_bias, tile_bias], axis=0)
    present = jnp.where(high > low, 1.0, 0.0)
    gates = jnp.tanh(gate[...])
    gate_at = lax.broadcasted_iota(jnp.int32, gates.shape, 1)

    def cross_head(kv_head, _):
        cols = pl.ds(pl.multiple_of(kv_head * HEAD_SIZE, 128), HEAD_SIZE)
        v_cols = pl.ds(pl.multiple_of(kv_cols + kv_head * HEAD_SIZE, 128), HEAD_SIZE)
        k, v = ikv[:, cols], ikv[:, v_cols]
        for pair in range(ratio // 2):
            at, two = query_pair(kv_head, pair)
            o = attend(two, k, v, tile_bias)
            for j in (0, 1):
                of = kv_head * ratio + 2 * pair + j
                t = jnp.sum(jnp.where(gate_at == of, gates, 0.0), axis=1, keepdims=True)
                where = pl.ds(at + j * HEAD_SIZE, HEAD_SIZE)
                total = self_out[:, where] + (t * present) * o[j * rows : (j + 1) * rows]
                out[:, where] = total.astype(BF16)
        return 0

    lax.fori_loop(0, kv_heads, cross_head, 0)

    send_wo.wait_send()
    send_va.wait_send()
    if ring:
        for c in cw + ccw + across:
            c.wait_send()
    for d, kv_copy, doc_copy in text:
        @pl.when(s + d < n)
        def _():
            kv_copy.wait_send()
            doc_copy.wait_send()

    @pl.when(s + 1 < n)
    def _():
        send_img.wait_send()

    @pl.when(s >= 1)
    def _():
        pass_img.wait_send()


def per_device(
    groups, n, text_query_rows, text_key_value, doc_ids, tile_span, vision_hidden, vision_qkv,
    vision_out_weight, cross_keyvalue_weight, cross_gate,
):
    rows, q_cols = text_query_rows.shape
    tile, width = vision_hidden.shape
    kv_cols = text_key_value.shape[2]
    part = vision_qkv.shape[2]
    shard = cross_keyvalue_weight.shape[0]
    ring = n == RING_PLACES and groups == 2 and shard % 32 == 0
    weight = cross_keyvalue_weight.reshape(shard, 2 * kv_cols)
    if not ring:
        weight = lax.all_gather(weight, "seq", axis=0, tiled=True)
    anywhere = pl.BlockSpec(memory_space=pl.ANY)
    vmem = pl.BlockSpec(memory_space=pltpu.VMEM)
    return pl.pallas_call(
        functools.partial(kernel, n, ring),
        out_shape=jax.ShapeDtypeStruct((rows, q_cols), BF16),
        in_specs=[anywhere, anywhere, vmem, vmem, vmem, anywhere, anywhere, anywhere, anywhere, vmem],
        out_specs=vmem,
        scratch_shapes=[
            pltpu.VMEM((rows, q_cols), BF16),
            pltpu.VMEM((2, 3 * rows, kv_cols), BF16),
            pltpu.VMEM((2, 1, rows), jnp.int32),
            pltpu.VMEM((tile, width), BF16),
            pltpu.VMEM((3, tile, part), BF16),
            pltpu.VMEM((2, part, width), BF16),
            pltpu.VMEM((width, 2 * kv_cols), BF16),
            pltpu.VMEM((2, tile, part), BF16),
            pltpu.VMEM((tile, width), F32),
            pltpu.VMEM((2 * tile, width), BF16),
            pltpu.VMEM((2 * tile, 2 * kv_cols), BF16),
            pltpu.VMEM((rows, q_cols), F32),
            pltpu.SemaphoreType.DMA((32,)),
            pltpu.SemaphoreType.DMA((32,)),
            pltpu.SemaphoreType.DMA((8,)),
        ],
        compiler_params=pltpu.CompilerParams(
            collective_id=0, has_side_effects=True, vmem_limit_bytes=48 * 1024 * 1024
        ),
    )(
        text_query_rows, text_key_value, doc_ids.reshape(1, rows), doc_ids.reshape(rows, 1),
        tile_span, vision_hidden, vision_qkv, vision_out_weight, weight,
        cross_gate.reshape(1, -1),
    )


def solution(mesh):
    placed = (
        P(("groups", "seq"), "head"),
        P(None, ("groups", "seq"), "head"),
        P(("groups", "seq")),
        P(("groups", "seq"), None),
        P(("groups", "seq"), None),
        P(None, ("groups", "seq"), "head"),
        P("head", None),
        P("seq", None, "head"),
        P("head"),
    )
    return jax.shard_map(
        functools.partial(per_device, mesh.shape["groups"], mesh.shape["seq"]),
        mesh=mesh,
        in_specs=placed,
        out_specs=P(("groups", "seq"), "head"),
        check_vma=False,
    )
```

```python
import functools
import math

import jax
import jax.numpy as jnp
from jax import lax
from jax.experimental import pallas as pl
from jax.experimental.pallas import tpu as pltpu
from jax.sharding import PartitionSpec as P

HEAD_SIZE = 128
VHD = 80
MESH = pl.DeviceIdType.MESH
BIG = -1e30
LOG2E = math.log2(math.e)
RING_PLACES = 8
SEMS = 56
SUBS = 2
OVER = 4
F32 = jnp.float32
BF16 = jnp.bfloat16


def dot_t(a, b):
    return lax.dot_general(a, b, (((1,), (1,)), ((), ())), preferred_element_type=F32)


def as_column(row):
    square = jnp.broadcast_to(row, (row.shape[1], row.shape[1]))
    return jnp.transpose(square)[:, 0:1]


def attend(q, k, v, bias):
    s = dot_t(q, k) * (LOG2E / math.sqrt(HEAD_SIZE)) + bias
    m = jnp.max(s, axis=-1, keepdims=True)
    p = jnp.exp2(s - m).astype(BF16)
    o = jnp.dot(p, jnp.concatenate([v, jnp.ones_like(v)], axis=1), preferred_element_type=F32)
    return o[:, :HEAD_SIZE] / o[:, HEAD_SIZE:]


def kernel(
    n, ring, q_hbm, tkv_hbm, doc_row, span, hid_hbm, vqkv_hbm, wo_hbm, w_hbm, gate,
    out,
    q, tkv, docs, hid, vqkv, wo, w, va, mix, img, ikv, self_out, sems, rsems, lsems,
):
    g, s, h = lax.axis_index("groups"), lax.axis_index("seq"), lax.axis_index("head")
    rows = q.shape[0]
    tile = hid.shape[0]
    half = tile // 2
    width = hid.shape[1]
    kv_cols = tkv.shape[2]
    kv_heads = kv_cols // HEAD_SIZE
    ratio = q.shape[1] // kv_cols
    shard = w_hbm.shape[0]
    part = vqkv.shape[2]
    counter = iter(range(SEMS))

    local = []

    def fetch(src, dst):
        c = pltpu.make_async_copy(src, dst, lsems.at[len(local)])
        c.start()
        local.append(c)
        return c

    def remote(src, dst, to):
        i = next(counter)
        return pltpu.make_async_remote_copy(
            src_ref=src, dst_ref=dst, send_sem=sems.at[i], recv_sem=rsems.at[i],
            device_id=to, device_id_type=MESH,
        )

    get_vqkv = fetch(vqkv_hbm, vqkv)
    get_wo = fetch(wo_hbm, wo.at[h])
    get_hid = fetch(hid_hbm, hid)
    my_rows = pl.ds(pl.multiple_of(s * shard, 16), shard) if ring else pl.ds(0, shard)
    get_w = fetch(w_hbm, w.at[my_rows])
    get_tkv = fetch(tkv_hbm, tkv.at[:, pl.ds(2 * rows, rows)])
    get_q = fetch(q_hbm, q)

    sibling = (g, s, 1 - h)
    barrier = pltpu.get_barrier_semaphore()

    def greet(to):
        pl.semaphore_signal(barrier, inc=1, device_id=to, device_id_type=MESH)

    greet(sibling)
    greets = 1
    if ring:
        place = jnp.where(s % 2 == 0, s // 2, RING_PLACES - 1 - s // 2)

        def at_place(r):
            r = (r + RING_PLACES) % RING_PLACES
            return jnp.where(r < RING_PLACES // 2, 2 * r, 2 * RING_PLACES - 1 - 2 * r)

        right, left = (g, at_place(place + 1), h), (g, at_place(place - 1), h)
        partner = (1 - g, s, h)
        for to in (right, left, partner):
            greet(to)
        greets = 4
    for d in (1, 2):
        @pl.when(s + d < n)
        def _():
            greet((g, jnp.minimum(s + d, n - 1), h))

        @pl.when(s - d >= 0)
        def _():
            greet((g, jnp.maximum(s - d, 0), h))
    near = sum(
        jnp.where(s + d < n, 1, 0) + jnp.where(s - d >= 0, 1, 0) for d in (1, 2)
    )
    pl.semaphore_wait(barrier, greets + near)

    if ring:
        over = shard // 16 * OVER // 10 * 16
        share = shard - over
        off = pl.multiple_of(g * over, 16)
        give = pl.multiple_of(g * share, 16)

        def piece(place_of, start, size):
            at = at_place(place_of) * shard + start
            return w.at[pl.ds(pl.multiple_of(at, 16), size)]

        size = share // SUBS
        right_way, left_way, across = {}, {}, []

    def ring_start(k, i):
        for way, to, back, turn in ((right_way, right, 1 - k, 0), (left_way, left, k - 1, 1)):
            if k < 4 or i % 2 == turn:
                dst = piece(place + back, off + i * size, size)
                src = w_hbm.at[pl.ds(pl.multiple_of(off + i * size, 16), size)] if k == 1 else dst
                way[k, i] = remote(src, dst, to)
                way[k, i].start()

    def ring_service(k):
        if not ring:
            return
        for i in range(SUBS):
            for way in (right_way, left_way):
                if (k, i) in way:
                    way[k, i].wait_recv()
            if k < 4:
                ring_start(k + 1, i)
        for at in (place - k, place + k)[: 1 if k == 4 else 2]:
            block = piece(at, give, over)
            across.append(remote(block, block, partner))
            across[-1].start()

    if ring:
        for i in range(SUBS):
            ring_start(1, i)
    send_wo = remote(wo_hbm, wo.at[h], sibling)
    send_wo.start()
    text = []
    for d in (1, 2):
        to = (g, jnp.minimum(s + d, n - 1), h)
        text.append((
            d,
            remote(tkv_hbm, tkv.at[:, pl.ds((2 - d) * rows, rows)], to),
            remote(doc_row, docs.at[2 - d], to),
        ))

        @pl.when(s + d < n)
        def _():
            text[-1][1].start()
            text[-1][2].start()

        @pl.when(s - d < 0)
        def _():
            tkv[:, (2 - d) * rows : (3 - d) * rows] = jnp.zeros((2, rows, kv_cols), BF16)
            docs[2 - d] = jnp.full((1, rows), -1, jnp.int32)

    @pl.when(s == 0)
    def _():
        img[:tile] = jnp.zeros((tile, width), BF16)

    get_vqkv.wait()
    column = lax.broadcasted_iota(jnp.int32, (tile, 256), 1)
    mix[:, :part] = jnp.zeros((tile, part), F32)
    for head in range(part // VHD):
        start = min(head * VHD // 128 * 128, part - 256)
        first = head * VHD - start
        mine = (column >= first) & (column < first + VHD)
        window = slice(start, start + 256)
        vq = jnp.where(mine, vqkv[0, :, window], jnp.zeros((), BF16))
        sc = dot_t(vq, vqkv[1, :, window]) * (LOG2E / math.sqrt(VHD))
        p = jnp.exp2(sc - jnp.max(sc, axis=-1, keepdims=True))
        p = (p * (1.0 / jnp.sum(p, axis=-1, keepdims=True))).astype(BF16)
        o = jnp.dot(p, vqkv[2, :, window], preferred_element_type=F32)
        mix[:, window] = mix[:, window] + jnp.where(mine, o, 0.0)
        if head == 3:
            ring_service(1)
    va[h] = mix[:, :part].astype(BF16)
    send_va = remote(va.at[h], va.at[h], sibling)
    send_va.start()

    get_wo.wait()
    get_hid.wait()
    mix[...] = hid[...].astype(F32) + jnp.dot(va[h], wo[h], preferred_element_type=F32)
    send_wo.wait_recv()
    send_va.wait_recv()
    mixed = mix[...] + jnp.dot(va[1 - h], wo[1 - h], preferred_element_type=F32)
    norm = mixed * lax.rsqrt(jnp.mean(mixed * mixed, axis=-1, keepdims=True) + 1e-5)
    img[tile:] = norm.astype(BF16)
    mine_prev = img.at[pl.ds(pl.multiple_of(h * half, 16), half)]
    send_img = remote(
        img.at[pl.ds(pl.multiple_of(tile + h * half, 16), half)], mine_prev,
        (g, jnp.minimum(s + 1, n - 1), h),
    )
    pass_img = remote(mine_prev, mine_prev, sibling)

    @pl.when(s + 1 < n)
    def _():
        send_img.start()

    ring_service(2)

    for d, kv_copy, doc_copy in text:
        @pl.when(s - d >= 0)
        def _():
            kv_copy.wait_recv()
            doc_copy.wait_recv()
    get_tkv.wait()
    get_q.wait()
    key_docs = jnp.concatenate([docs[0], docs[1], doc_row[...]], axis=1)
    key_at = lax.broadcasted_iota(jnp.int32, (rows, 3 * rows), 1) - 2 * rows
    query_at = lax.broadcasted_iota(jnp.int32, (rows, 3 * rows), 0)
    seen = (key_docs == as_column(doc_row[...])) & (key_at <= query_at) & (key_at + s * rows >= 0)
    bias = jnp.where(seen, 0.0, BIG)
    bias = jnp.concatenate([bias, bias], axis=0)

    def query_pair(kv_head, pair):
        at = pl.multiple_of((kv_head * ratio + 2 * pair) * HEAD_SIZE, 128)
        return at, jnp.concatenate(
            [q[:, pl.ds(at, HEAD_SIZE)], q[:, pl.ds(at + HEAD_SIZE, HEAD_SIZE)]], axis=0
        )

    def self_head(kv_head, _):
        cols = pl.ds(pl.multiple_of(kv_head * HEAD_SIZE, 128), HEAD_SIZE)
        k, v = tkv[0, :, cols], tkv[1, :, cols]
        for pair in range(ratio // 2):
            at, two = query_pair(kv_head, pair)
            o = attend(two, k, v, bias)
            self_out[:, pl.ds(at, HEAD_SIZE)] = o[:rows]
            self_out[:, pl.ds(at + HEAD_SIZE, HEAD_SIZE)] = o[rows:]
        return 0

    lax.fori_loop(0, kv_heads // 2, self_head, 0)
    ring_service(3)

    @pl.when(s >= 1)
    def _():
        send_img.wait_recv()
        pass_img.start()

    lax.fori_loop(kv_heads // 2, kv_heads, self_head, 0)
    ring_service(4)

    @pl.when(s >= 1)
    def _():
        pass_img.wait_recv()

    get_w.wait()
    if ring:
        for c in across:
            c.wait_recv()

    def project(i, _):
        cols = pl.ds(pl.multiple_of(i * 256, 256), 256)
        ikv[:, cols] = jnp.dot(img[...], w[:, cols], preferred_element_type=F32).astype(BF16)
        return 0

    lax.fori_loop(0, ikv.shape[1] // 256, project, 0)

    low, high = as_column(span[0:1, :]), as_column(span[1:2, :])
    tile_of = s - 1 + lax.broadcasted_iota(jnp.int32, (rows, 2 * tile), 1) // tile
    seen_tiles = (tile_of >= low) & (tile_of < high)
    tile_bias = jnp.where(seen_tiles, 0.0, BIG)
    tile_bias = jnp.concatenate([tile_bias, tile_bias], axis=0)
    present = jnp.where(high > low, 1.0, 0.0)
    gates = jnp.tanh(gate[...])
    gate_at = lax.broadcasted_iota(jnp.int32, gates.shape, 1)

    def cross_head(kv_head, _):
        cols = pl.ds(pl.multiple_of(kv_head * HEAD_SIZE, 128), HEAD_SIZE)
        v_cols = pl.ds(pl.multiple_of(kv_cols + kv_head * HEAD_SIZE, 128), HEAD_SIZE)
        k, v = ikv[:, cols], ikv[:, v_cols]
        for pair in range(ratio // 2):
            at, two = query_pair(kv_head, pair)
            o = attend(two, k, v, tile_bias)
            for j in (0, 1):
                of = kv_head * ratio + 2 * pair + j
                t = jnp.sum(jnp.where(gate_at == of, gates, 0.0), axis=1, keepdims=True)
                where = pl.ds(at + j * HEAD_SIZE, HEAD_SIZE)
                total = self_out[:, where] + (t * present) * o[j * rows : (j + 1) * rows]
                out[:, where] = total.astype(BF16)
        return 0

    lax.fori_loop(0, kv_heads, cross_head, 0)

    send_wo.wait_send()
    send_va.wait_send()
    if ring:
        for c in [*right_way.values(), *left_way.values(), *across]:
            c.wait_send()
    for d, kv_copy, doc_copy in text:
        @pl.when(s + d < n)
        def _():
            kv_copy.wait_send()
            doc_copy.wait_send()

    @pl.when(s + 1 < n)
    def _():
        send_img.wait_send()

    @pl.when(s >= 1)
    def _():
        pass_img.wait_send()


def per_device(
    groups, n, text_query_rows, text_key_value, doc_ids, tile_span, vision_hidden, vision_qkv,
    vision_out_weight, cross_keyvalue_weight, cross_gate,
):
    rows, q_cols = text_query_rows.shape
    tile, width = vision_hidden.shape
    kv_cols = text_key_value.shape[2]
    part = vision_qkv.shape[2]
    shard = cross_keyvalue_weight.shape[0]
    ring = n == RING_PLACES and groups == 2 and shard % 160 == 0
    weight = cross_keyvalue_weight.reshape(shard, 2 * kv_cols)
    if not ring:
        weight = lax.all_gather(weight, "seq", axis=0, tiled=True)
    anywhere = pl.BlockSpec(memory_space=pl.ANY)
    vmem = pl.BlockSpec(memory_space=pltpu.VMEM)
    return pl.pallas_call(
        functools.partial(kernel, n, ring),
        out_shape=jax.ShapeDtypeStruct((rows, q_cols), BF16),
        in_specs=[anywhere, anywhere, vmem, vmem, anywhere, anywhere, anywhere, anywhere, vmem],
        out_specs=vmem,
        scratch_shapes=[
            pltpu.VMEM((rows, q_cols), BF16),
            pltpu.VMEM((2, 3 * rows, kv_cols), BF16),
            pltpu.VMEM((2, 1, rows), jnp.int32),
            pltpu.VMEM((tile, width), BF16),
            pltpu.VMEM((3, tile, part), BF16),
            pltpu.VMEM((2, part, width), BF16),
            pltpu.VMEM((width, 2 * kv_cols), BF16),
            pltpu.VMEM((2, tile, part), BF16),
            pltpu.VMEM((tile, width), F32),
            pltpu.VMEM((2 * tile, width), BF16),
            pltpu.VMEM((2 * tile, 2 * kv_cols), BF16),
            pltpu.VMEM((rows, q_cols), F32),
            pltpu.SemaphoreType.DMA((SEMS,)),
            pltpu.SemaphoreType.DMA((SEMS,)),
            pltpu.SemaphoreType.DMA((8,)),
        ],
        compiler_params=pltpu.CompilerParams(
            collective_id=0, has_side_effects=True, vmem_limit_bytes=62 * 1024 * 1024
        ),
    )(
        text_query_rows, text_key_value, doc_ids.reshape(1, rows), tile_span.T,
        vision_hidden, vision_qkv, vision_out_weight, weight,
        cross_gate.reshape(1, -1),
    )


def solution(mesh):
    placed = (
        P(("groups", "seq"), "head"),
        P(None, ("groups", "seq"), "head"),
        P(("groups", "seq")),
        P(("groups", "seq"), None),
        P(("groups", "seq"), None),
        P(None, ("groups", "seq"), "head"),
        P("head", None),
        P("seq", None, "head"),
        P("head"),
    )
    return jax.shard_map(
        functools.partial(per_device, mesh.shape["groups"], mesh.shape["seq"]),
        mesh=mesh,
        in_specs=placed,
        out_specs=P(("groups", "seq"), "head"),
        check_vma=False,
    )
```

```python
import functools
import math

import jax
import jax.numpy as jnp
from jax import lax
from jax.experimental import pallas as pl
from jax.experimental.pallas import tpu as pltpu
from jax.sharding import PartitionSpec as P

HEAD_SIZE = 128
VHD = 80
MESH = pl.DeviceIdType.MESH
BIG = -1e30
LOG2E = math.log2(math.e)
RING_PLACES = 8
SEMS = 56
SUBS = 5
OVER = 5
F32 = jnp.float32
BF16 = jnp.bfloat16


def dot_t(a, b):
    return lax.dot_general(a, b, (((1,), (1,)), ((), ())), preferred_element_type=F32)


def as_column(row):
    square = jnp.broadcast_to(row, (row.shape[1], row.shape[1]))
    return jnp.transpose(square)[:, 0:1]


def attend(q, k, v, bias):
    s = dot_t(q, k) * (LOG2E / math.sqrt(HEAD_SIZE)) + bias
    m = jnp.max(s, axis=-1, keepdims=True)
    p = jnp.exp2(s - m).astype(BF16)
    o = jnp.dot(p, jnp.concatenate([v, jnp.ones_like(v)], axis=1), preferred_element_type=F32)
    return o[:, :HEAD_SIZE] / o[:, HEAD_SIZE:]


def kernel(
    n, ring, q_hbm, tkv_hbm, doc_row, span, hid_hbm, vqkv_hbm, wo_hbm, w_hbm, gate,
    out,
    q, tkv, docs, hid, vqkv, wo, w, va, mix, img, ikv, self_out, sems, rsems, lsems,
):
    g, s, h = lax.axis_index("groups"), lax.axis_index("seq"), lax.axis_index("head")
    rows = q.shape[0]
    tile = hid.shape[0]
    half = tile // 2
    width = hid.shape[1]
    kv_cols = tkv.shape[2]
    kv_heads = kv_cols // HEAD_SIZE
    ratio = q.shape[1] // kv_cols
    shard = w_hbm.shape[0]
    part = vqkv.shape[2]
    counter = iter(range(SEMS))

    local = []

    def fetch(src, dst):
        c = pltpu.make_async_copy(src, dst, lsems.at[len(local)])
        c.start()
        local.append(c)
        return c

    def remote(src, dst, to):
        i = next(counter)
        return pltpu.make_async_remote_copy(
            src_ref=src, dst_ref=dst, send_sem=sems.at[i], recv_sem=rsems.at[i],
            device_id=to, device_id_type=MESH,
        )

    get_vqkv = fetch(vqkv_hbm, vqkv)
    get_wo = fetch(wo_hbm, wo.at[h])
    get_hid = fetch(hid_hbm, hid)
    my_rows = pl.ds(pl.multiple_of(s * shard, 16), shard) if ring else pl.ds(0, shard)
    get_w = fetch(w_hbm, w.at[my_rows])
    get_tkv = fetch(tkv_hbm, tkv.at[:, pl.ds(2 * rows, rows)])
    get_q = fetch(q_hbm, q)

    sibling = (g, s, 1 - h)
    barrier = pltpu.get_barrier_semaphore()

    def greet(to):
        pl.semaphore_signal(barrier, inc=1, device_id=to, device_id_type=MESH)

    greet(sibling)
    greets = 1
    if ring:
        place = jnp.where(s % 2 == 0, s // 2, RING_PLACES - 1 - s // 2)

        def at_place(r):
            r = (r + RING_PLACES) % RING_PLACES
            return jnp.where(r < RING_PLACES // 2, 2 * r, 2 * RING_PLACES - 1 - 2 * r)

        right, left = (g, at_place(place + 1), h), (g, at_place(place - 1), h)
        partner = (1 - g, s, h)
        for to in (right, left, partner):
            greet(to)
        greets = 4
    for d in (1, 2):
        @pl.when(s + d < n)
        def _():
            greet((g, jnp.minimum(s + d, n - 1), h))

        @pl.when(s - d >= 0)
        def _():
            greet((g, jnp.maximum(s - d, 0), h))
    near = sum(
        jnp.where(s + d < n, 1, 0) + jnp.where(s - d >= 0, 1, 0) for d in (1, 2)
    )
    pl.semaphore_wait(barrier, greets + near)

    if ring:
        over = shard // 16 * OVER // 10 * 16
        share = shard - over
        off = pl.multiple_of(g * over, 16)
        give = pl.multiple_of(g * share, 16)

        def piece(place_of, start, size):
            at = at_place(place_of) * shard + start
            return w.at[pl.ds(pl.multiple_of(at, 16), size)]

        size = share // SUBS
        right_way, left_way, across = {}, {}, []

    def ring_start(k, i):
        for way, to, back, turn in ((right_way, right, 1 - k, 0), (left_way, left, k - 1, 1)):
            if k < 4 or i % 2 == turn:
                dst = piece(place + back, off + i * size, size)
                src = w_hbm.at[pl.ds(pl.multiple_of(off + i * size, 16), size)] if k == 1 else dst
                way[k, i] = remote(src, dst, to)
                way[k, i].start()

    def ring_service(k):
        if not ring:
            return
        for i in range(SUBS):
            for way in (right_way, left_way):
                if (k, i) in way:
                    way[k, i].wait_recv()
            if k < 4:
                ring_start(k + 1, i)
        for at in (place - k, place + k)[: 1 if k == 4 else 2]:
            block = piece(at, give, over)
            across.append(remote(block, block, partner))
            across[-1].start()

    if ring:
        for i in range(SUBS):
            ring_start(1, i)
    send_wo = remote(wo_hbm, wo.at[h], sibling)
    send_wo.start()
    far = remote(tkv_hbm, tkv.at[:, pl.ds(0, rows)], (g, jnp.minimum(s + 2, n - 1), h))
    odd = s % 2
    turned = n % 2 == 0
    step = 1 - 2 * odd
    near_to = jnp.clip(s + step, 0, n - 1) if turned else jnp.minimum(s + 1, n - 1)
    middle = tkv.at[:, pl.ds(rows, rows)]
    close = remote(tkv_hbm, middle, (g, near_to, h))
    back = remote(tkv.at[:, pl.ds(0, rows)], middle, (g, near_to, h))
    ids = [
        remote(doc_row, docs.at[2 - d], (g, jnp.minimum(s + d, n - 1), h)) for d in (1, 2)
    ]
    has_close = odd == 0 if turned else s + 1 < n
    has_back = (odd == 1) & (s >= 2) if turned else s < 0

    @pl.when(s + 2 < n)
    def _():
        far.start()

    @pl.when(has_close)
    def _():
        close.start()

    for d in (1, 2):
        @pl.when(s + d < n)
        def _():
            ids[d - 1].start()

        @pl.when(s - d < 0)
        def _():
            tkv[:, (2 - d) * rows : (3 - d) * rows] = jnp.zeros((2, rows, kv_cols), BF16)
            docs[2 - d] = jnp.full((1, rows), -1, jnp.int32)

    @pl.when(s == 0)
    def _():
        img[:tile] = jnp.zeros((tile, width), BF16)

    get_vqkv.wait()
    column = lax.broadcasted_iota(jnp.int32, (tile, 256), 1)
    mix[:, :part] = jnp.zeros((tile, part), F32)
    for head in range(part // VHD):
        start = min(head * VHD // 128 * 128, part - 256)
        first = head * VHD - start
        mine = (column >= first) & (column < first + VHD)
        window = slice(start, start + 256)
        vq = jnp.where(mine, vqkv[0, :, window], jnp.zeros((), BF16))
        sc = dot_t(vq, vqkv[1, :, window]) * (LOG2E / math.sqrt(VHD))
        p = jnp.exp2(sc - jnp.max(sc, axis=-1, keepdims=True))
        p = (p * (1.0 / jnp.sum(p, axis=-1, keepdims=True))).astype(BF16)
        o = jnp.dot(p, vqkv[2, :, window], preferred_element_type=F32)
        mix[:, window] = mix[:, window] + jnp.where(mine, o, 0.0)
        if head == 3:
            ring_service(1)
    va[h] = mix[:, :part].astype(BF16)
    send_va = remote(va.at[h], va.at[h], sibling)
    send_va.start()

    get_wo.wait()
    get_hid.wait()
    mix[...] = hid[...].astype(F32) + jnp.dot(va[h], wo[h], preferred_element_type=F32)
    send_wo.wait_recv()
    send_va.wait_recv()
    mixed = mix[...] + jnp.dot(va[1 - h], wo[1 - h], preferred_element_type=F32)
    norm = mixed * lax.rsqrt(jnp.mean(mixed * mixed, axis=-1, keepdims=True) + 1e-5)
    img[tile:] = norm.astype(BF16)
    mine_prev = img.at[pl.ds(pl.multiple_of(h * half, 16), half)]
    send_img = remote(
        img.at[pl.ds(pl.multiple_of(tile + h * half, 16), half)], mine_prev,
        (g, jnp.minimum(s + 1, n - 1), h),
    )
    pass_img = remote(mine_prev, mine_prev, sibling)

    @pl.when(s + 1 < n)
    def _():
        send_img.start()

    ring_service(2)

    @pl.when(s >= 2)
    def _():
        far.wait_recv()
        ids[1].wait_recv()

    @pl.when(has_back)
    def _():
        back.start()

    @pl.when(s >= 1)
    def _():
        ids[0].wait_recv()

    ring_service(3)
    ring_service(4)

    @pl.when(s >= 1)
    def _():
        send_img.wait_recv()
        pass_img.start()

    if turned:
        @pl.when(odd == 1)
        def _():
            close.wait_recv()

        @pl.when((odd == 0) & (s >= 2))
        def _():
            back.wait_recv()
    else:
        @pl.when(s >= 1)
        def _():
            close.wait_recv()
    get_tkv.wait()
    get_q.wait()
    key_docs = jnp.concatenate([docs[0], docs[1], doc_row[...]], axis=1)
    key_at = lax.broadcasted_iota(jnp.int32, (rows, 3 * rows), 1) - 2 * rows
    query_at = lax.broadcasted_iota(jnp.int32, (rows, 3 * rows), 0)
    seen = (key_docs == as_column(doc_row[...])) & (key_at <= query_at) & (key_at + s * rows >= 0)
    bias = jnp.where(seen, 0.0, BIG)
    bias = jnp.concatenate([bias, bias], axis=0)

    def query_pair(kv_head, pair):
        at = pl.multiple_of((kv_head * ratio + 2 * pair) * HEAD_SIZE, 128)
        return at, jnp.concatenate(
            [q[:, pl.ds(at, HEAD_SIZE)], q[:, pl.ds(at + HEAD_SIZE, HEAD_SIZE)]], axis=0
        )

    def self_head(kv_head, _):
        cols = pl.ds(pl.multiple_of(kv_head * HEAD_SIZE, 128), HEAD_SIZE)
        k, v = tkv[0, :, cols], tkv[1, :, cols]
        for pair in range(ratio // 2):
            at, two = query_pair(kv_head, pair)
            o = attend(two, k, v, bias)
            self_out[:, pl.ds(at, HEAD_SIZE)] = o[:rows]
            self_out[:, pl.ds(at + HEAD_SIZE, HEAD_SIZE)] = o[rows:]
        return 0


    lax.fori_loop(0, kv_heads, self_head, 0)

    @pl.when(s >= 1)
    def _():
        pass_img.wait_recv()

    get_w.wait()
    if ring:
        for c in across:
            c.wait_recv()

    def project(i, _):
        cols = pl.ds(pl.multiple_of(i * 256, 256), 256)
        ikv[:, cols] = jnp.dot(img[...], w[:, cols], preferred_element_type=F32).astype(BF16)
        return 0

    lax.fori_loop(0, ikv.shape[1] // 256, project, 0)

    low, high = as_column(span[0:1, :]), as_column(span[1:2, :])
    tile_of = s - 1 + lax.broadcasted_iota(jnp.int32, (rows, 2 * tile), 1) // tile
    seen_tiles = (tile_of >= low) & (tile_of < high)
    tile_bias = jnp.where(seen_tiles, 0.0, BIG)
    tile_bias = jnp.concatenate([tile_bias, tile_bias], axis=0)
    present = jnp.where(high > low, 1.0, 0.0)
    gates = jnp.tanh(gate[...])
    gate_at = lax.broadcasted_iota(jnp.int32, gates.shape, 1)

    def cross_head(kv_head, _):
        cols = pl.ds(pl.multiple_of(kv_head * HEAD_SIZE, 128), HEAD_SIZE)
        v_cols = pl.ds(pl.multiple_of(kv_cols + kv_head * HEAD_SIZE, 128), HEAD_SIZE)
        k, v = ikv[:, cols], ikv[:, v_cols]
        for pair in range(ratio // 2):
            at, two = query_pair(kv_head, pair)
            o = attend(two, k, v, tile_bias)
            for j in (0, 1):
                of = kv_head * ratio + 2 * pair + j
                t = jnp.sum(jnp.where(gate_at == of, gates, 0.0), axis=1, keepdims=True)
                where = pl.ds(at + j * HEAD_SIZE, HEAD_SIZE)
                total = self_out[:, where] + (t * present) * o[j * rows : (j + 1) * rows]
                out[:, where] = total.astype(BF16)
        return 0

    lax.fori_loop(0, kv_heads, cross_head, 0)

    send_wo.wait_send()
    send_va.wait_send()
    if ring:
        for c in [*right_way.values(), *left_way.values(), *across]:
            c.wait_send()
    for d in (1, 2):
        @pl.when(s + d < n)
        def _():
            ids[d - 1].wait_send()

    @pl.when(s + 2 < n)
    def _():
        far.wait_send()

    @pl.when(has_close)
    def _():
        close.wait_send()

    @pl.when(has_back)
    def _():
        back.wait_send()

    @pl.when(s + 1 < n)
    def _():
        send_img.wait_send()

    @pl.when(s >= 1)
    def _():
        pass_img.wait_send()


def per_device(
    groups, n, text_query_rows, text_key_value, doc_ids, tile_span, vision_hidden, vision_qkv,
    vision_out_weight, cross_keyvalue_weight, cross_gate,
):
    rows, q_cols = text_query_rows.shape
    tile, width = vision_hidden.shape
    kv_cols = text_key_value.shape[2]
    part = vision_qkv.shape[2]
    shard = cross_keyvalue_weight.shape[0]
    ring = n == RING_PLACES and groups == 2 and shard % 160 == 0
    weight = cross_keyvalue_weight.reshape(shard, 2 * kv_cols)
    if not ring:
        weight = lax.all_gather(weight, "seq", axis=0, tiled=True)
    anywhere = pl.BlockSpec(memory_space=pl.ANY)
    vmem = pl.BlockSpec(memory_space=pltpu.VMEM)
    return pl.pallas_call(
        functools.partial(kernel, n, ring),
        out_shape=jax.ShapeDtypeStruct((rows, q_cols), BF16),
        in_specs=[anywhere, anywhere, vmem, vmem, anywhere, anywhere, anywhere, anywhere, vmem],
        out_specs=vmem,
        scratch_shapes=[
            pltpu.VMEM((rows, q_cols), BF16),
            pltpu.VMEM((2, 3 * rows, kv_cols), BF16),
            pltpu.VMEM((2, 1, rows), jnp.int32),
            pltpu.VMEM((tile, width), BF16),
            pltpu.VMEM((3, tile, part), BF16),
            pltpu.VMEM((2, part, width), BF16),
            pltpu.VMEM((width, 2 * kv_cols), BF16),
            pltpu.VMEM((2, tile, part), BF16),
            pltpu.VMEM((tile, width), F32),
            pltpu.VMEM((2 * tile, width), BF16),
            pltpu.VMEM((2 * tile, 2 * kv_cols), BF16),
            pltpu.VMEM((rows, q_cols), F32),
            pltpu.SemaphoreType.DMA((SEMS,)),
            pltpu.SemaphoreType.DMA((SEMS,)),
            pltpu.SemaphoreType.DMA((8,)),
        ],
        compiler_params=pltpu.CompilerParams(
            collective_id=0, has_side_effects=True, vmem_limit_bytes=62 * 1024 * 1024
        ),
    )(
        text_query_rows, text_key_value, doc_ids.reshape(1, rows), tile_span.T,
        vision_hidden, vision_qkv, vision_out_weight, weight,
        cross_gate.reshape(1, -1),
    )


def solution(mesh):
    placed = (
        P(("groups", "seq"), "head"),
        P(None, ("groups", "seq"), "head"),
        P(("groups", "seq")),
        P(("groups", "seq"), None),
        P(("groups", "seq"), None),
        P(None, ("groups", "seq"), "head"),
        P("head", None),
        P("seq", None, "head"),
        P("head"),
    )
    return jax.shard_map(
        functools.partial(per_device, mesh.shape["groups"], mesh.shape["seq"]),
        mesh=mesh,
        in_specs=placed,
        out_specs=P(("groups", "seq"), "head"),
        check_vma=False,
    )
```

```python
import functools
import math

import jax
import jax.numpy as jnp
from jax import lax
from jax.experimental import pallas as pl
from jax.experimental.pallas import tpu as pltpu
from jax.sharding import PartitionSpec as P

HEAD_SIZE = 128
VHD = 80
MESH = pl.DeviceIdType.MESH
BIG = -1e30
LOG2E = math.log2(math.e)
RING_PLACES = 8
SEMS = 96
SUBS = 5
F32 = jnp.float32
BF16 = jnp.bfloat16


def dot_t(a, b):
    return lax.dot_general(a, b, (((1,), (1,)), ((), ())), preferred_element_type=F32)


def as_column(row):
    square = jnp.broadcast_to(row, (row.shape[1], row.shape[1]))
    return jnp.transpose(square)[:, 0:1]


def attend(q, k, v, bias):
    s = dot_t(q, k) * (LOG2E / math.sqrt(HEAD_SIZE)) + bias
    m = jnp.max(s, axis=-1, keepdims=True)
    p = jnp.exp2(s - m).astype(BF16)
    o = jnp.dot(p, jnp.concatenate([v, jnp.ones_like(v)], axis=1), preferred_element_type=F32)
    return o[:, :HEAD_SIZE] / o[:, HEAD_SIZE:]


def kernel(
    n, ring, q_hbm, tkv_hbm, doc_row, span, hid_hbm, vqkv_hbm, wo_hbm, w_hbm, gate,
    out,
    q, tkv, docs, hid, vqkv, wo, w, va, mix, img, ikv, self_out, sems, rsems, lsems,
):
    g, s, h = lax.axis_index("groups"), lax.axis_index("seq"), lax.axis_index("head")
    rows = q.shape[0]
    tile = hid.shape[0]
    half = tile // 2
    width = hid.shape[1]
    kv_cols = tkv.shape[2]
    kv_heads = kv_cols // HEAD_SIZE
    ratio = q.shape[1] // kv_cols
    shard = w_hbm.shape[0]
    part = vqkv.shape[2]
    counter = iter(range(SEMS))

    local = []

    def fetch(src, dst):
        c = pltpu.make_async_copy(src, dst, lsems.at[len(local)])
        c.start()
        local.append(c)
        return c

    def remote(src, dst, to):
        i = next(counter)
        return pltpu.make_async_remote_copy(
            src_ref=src, dst_ref=dst, send_sem=sems.at[i], recv_sem=rsems.at[i],
            device_id=to, device_id_type=MESH,
        )

    get_vqkv = fetch(vqkv_hbm, vqkv)
    get_wo = fetch(wo_hbm, wo.at[h])
    get_hid = fetch(hid_hbm, hid)
    my_rows = pl.ds(pl.multiple_of(s * shard, 16), shard) if ring else pl.ds(0, shard)
    get_w = fetch(w_hbm, w.at[my_rows])
    get_tkv = fetch(tkv_hbm, tkv.at[:, pl.ds(2 * rows, rows)])
    get_q = fetch(q_hbm, q)

    sibling = (g, s, 1 - h)
    barrier = pltpu.get_barrier_semaphore()

    def greet(to):
        pl.semaphore_signal(barrier, inc=1, device_id=to, device_id_type=MESH)

    greet(sibling)
    greets = 1
    if ring:
        place = jnp.where(s % 2 == 0, s // 2, RING_PLACES - 1 - s // 2)

        def at_place(r):
            r = (r + RING_PLACES) % RING_PLACES
            return jnp.where(r < RING_PLACES // 2, 2 * r, 2 * RING_PLACES - 1 - 2 * r)

        right, left = (g, at_place(place + 1), h), (g, at_place(place - 1), h)
        partner = (1 - g, s, h)
        for to in (right, left, partner):
            greet(to)
        greets = 4
    for d in (1, 2):
        @pl.when(s + d < n)
        def _():
            greet((g, jnp.minimum(s + d, n - 1), h))

        @pl.when(s - d >= 0)
        def _():
            greet((g, jnp.maximum(s - d, 0), h))
    near = sum(
        jnp.where(s + d < n, 1, 0) + jnp.where(s - d >= 0, 1, 0) for d in (1, 2)
    )
    pl.semaphore_wait(barrier, greets + near)

    if ring:
        over = shard // 2
        share = shard - over
        off = pl.multiple_of(g * over, 16)

        def piece(place_of, start, size):
            at = at_place(place_of) * shard + start
            return w.at[pl.ds(pl.multiple_of(at, 16), size)]

        size = share // SUBS
        right_way, left_way, across = {}, {}, []

    def ring_start(k, i):
        for way, to, back, turn in ((right_way, right, 1 - k, 0), (left_way, left, k - 1, 1)):
            if k < 4 or i % 2 == turn:
                dst = piece(place + back, off + i * size, size)
                src = w_hbm.at[pl.ds(pl.multiple_of(off + i * size, 16), size)] if k == 1 else dst
                way[k, i] = remote(src, dst, to)
                way[k, i].start()

    def ring_service(k):
        if not ring:
            return
        for i in range(SUBS):
            for way, at in ((right_way, place - k), (left_way, place + k)):
                if (k, i) in way:
                    way[k, i].wait_recv()
                    block = piece(at, off + i * size, size)
                    across.append(remote(block, block, partner))
                    across[-1].start()
            if k < 4:
                ring_start(k + 1, i)

    if ring:
        for i in range(SUBS):
            ring_start(1, i)
    send_wo = remote(wo_hbm, wo.at[h], sibling)
    send_wo.start()
    far = remote(tkv_hbm, tkv.at[:, pl.ds(0, rows)], (g, jnp.minimum(s + 2, n - 1), h))
    odd = s % 2
    turned = n % 2 == 0
    step = 1 - 2 * odd
    near_to = jnp.clip(s + step, 0, n - 1) if turned else jnp.minimum(s + 1, n - 1)
    middle = tkv.at[:, pl.ds(rows, rows)]
    close = remote(tkv_hbm, middle, (g, near_to, h))
    back = remote(tkv.at[:, pl.ds(0, rows)], middle, (g, near_to, h))
    ids = [
        remote(doc_row, docs.at[2 - d], (g, jnp.minimum(s + d, n - 1), h)) for d in (1, 2)
    ]
    has_close = odd == 0 if turned else s + 1 < n
    has_back = (odd == 1) & (s >= 2) if turned else s < 0

    @pl.when(s + 2 < n)
    def _():
        far.start()

    @pl.when(has_close)
    def _():
        close.start()

    for d in (1, 2):
        @pl.when(s + d < n)
        def _():
            ids[d - 1].start()

        @pl.when(s - d < 0)
        def _():
            tkv[:, (2 - d) * rows : (3 - d) * rows] = jnp.zeros((2, rows, kv_cols), BF16)
            docs[2 - d] = jnp.full((1, rows), -1, jnp.int32)

    @pl.when(s == 0)
    def _():
        img[:tile] = jnp.zeros((tile, width), BF16)

    get_vqkv.wait()
    column = lax.broadcasted_iota(jnp.int32, (tile, 256), 1)
    mix[:, :part] = jnp.zeros((tile, part), F32)
    for head in range(part // VHD):
        start = min(head * VHD // 128 * 128, part - 256)
        first = head * VHD - start
        mine = (column >= first) & (column < first + VHD)
        window = slice(start, start + 256)
        vq = jnp.where(mine, vqkv[0, :, window], jnp.zeros((), BF16))
        sc = dot_t(vq, vqkv[1, :, window]) * (LOG2E / math.sqrt(VHD))
        p = jnp.exp2(sc - jnp.max(sc, axis=-1, keepdims=True))
        p = (p * (1.0 / jnp.sum(p, axis=-1, keepdims=True))).astype(BF16)
        o = jnp.dot(p, vqkv[2, :, window], preferred_element_type=F32)
        mix[:, window] = mix[:, window] + jnp.where(mine, o, 0.0)
        if head == 3:
            ring_service(1)
    va[h] = mix[:, :part].astype(BF16)
    send_va = remote(va.at[h], va.at[h], sibling)
    send_va.start()

    get_wo.wait()
    get_hid.wait()
    mix[...] = hid[...].astype(F32) + jnp.dot(va[h], wo[h], preferred_element_type=F32)
    send_wo.wait_recv()
    send_va.wait_recv()
    mixed = mix[...] + jnp.dot(va[1 - h], wo[1 - h], preferred_element_type=F32)
    norm = mixed * lax.rsqrt(jnp.mean(mixed * mixed, axis=-1, keepdims=True) + 1e-5)
    img[tile:] = norm.astype(BF16)
    mine_prev = img.at[pl.ds(pl.multiple_of(h * half, 16), half)]
    send_img = remote(
        img.at[pl.ds(pl.multiple_of(tile + h * half, 16), half)], mine_prev,
        (g, jnp.minimum(s + 1, n - 1), h),
    )
    pass_img = remote(mine_prev, mine_prev, sibling)

    @pl.when(s + 1 < n)
    def _():
        send_img.start()

    ring_service(2)

    @pl.when(s >= 2)
    def _():
        far.wait_recv()
        ids[1].wait_recv()

    @pl.when(has_back)
    def _():
        back.start()

    @pl.when(s >= 1)
    def _():
        ids[0].wait_recv()

    ring_service(3)
    ring_service(4)

    @pl.when(s >= 1)
    def _():
        send_img.wait_recv()
        pass_img.start()

    if turned:
        @pl.when(odd == 1)
        def _():
            close.wait_recv()

        @pl.when((odd == 0) & (s >= 2))
        def _():
            back.wait_recv()
    else:
        @pl.when(s >= 1)
        def _():
            close.wait_recv()
    get_tkv.wait()
    get_q.wait()
    key_docs = jnp.concatenate([docs[0], docs[1], doc_row[...]], axis=1)
    key_at = lax.broadcasted_iota(jnp.int32, (rows, 3 * rows), 1) - 2 * rows
    query_at = lax.broadcasted_iota(jnp.int32, (rows, 3 * rows), 0)
    seen = (key_docs == as_column(doc_row[...])) & (key_at <= query_at) & (key_at + s * rows >= 0)
    bias = jnp.where(seen, 0.0, BIG)
    bias = jnp.concatenate([bias, bias], axis=0)

    def query_pair(kv_head, pair):
        at = pl.multiple_of((kv_head * ratio + 2 * pair) * HEAD_SIZE, 128)
        return at, jnp.concatenate(
            [q[:, pl.ds(at, HEAD_SIZE)], q[:, pl.ds(at + HEAD_SIZE, HEAD_SIZE)]], axis=0
        )

    def self_head(kv_head, _):
        cols = pl.ds(pl.multiple_of(kv_head * HEAD_SIZE, 128), HEAD_SIZE)
        k, v = tkv[0, :, cols], tkv[1, :, cols]
        for pair in range(ratio // 2):
            at, two = query_pair(kv_head, pair)
            o = attend(two, k, v, bias)
            self_out[:, pl.ds(at, HEAD_SIZE)] = o[:rows]
            self_out[:, pl.ds(at + HEAD_SIZE, HEAD_SIZE)] = o[rows:]
        return 0


    lax.fori_loop(0, kv_heads, self_head, 0)

    @pl.when(s >= 1)
    def _():
        pass_img.wait_recv()

    get_w.wait()
    if ring:
        for c in across:
            c.wait_recv()

    def project(i, _):
        cols = pl.ds(pl.multiple_of(i * 256, 256), 256)
        ikv[:, cols] = jnp.dot(img[...], w[:, cols], preferred_element_type=F32).astype(BF16)
        return 0

    lax.fori_loop(0, ikv.shape[1] // 256, project, 0)

    low, high = as_column(span[0:1, :]), as_column(span[1:2, :])
    tile_of = s - 1 + lax.broadcasted_iota(jnp.int32, (rows, 2 * tile), 1) // tile
    seen_tiles = (tile_of >= low) & (tile_of < high)
    tile_bias = jnp.where(seen_tiles, 0.0, BIG)
    tile_bias = jnp.concatenate([tile_bias, tile_bias], axis=0)
    present = jnp.where(high > low, 1.0, 0.0)
    gates = jnp.tanh(gate[...])
    gate_at = lax.broadcasted_iota(jnp.int32, gates.shape, 1)

    def cross_head(kv_head, _):
        cols = pl.ds(pl.multiple_of(kv_head * HEAD_SIZE, 128), HEAD_SIZE)
        v_cols = pl.ds(pl.multiple_of(kv_cols + kv_head * HEAD_SIZE, 128), HEAD_SIZE)
        k, v = ikv[:, cols], ikv[:, v_cols]
        for pair in range(ratio // 2):
            at, two = query_pair(kv_head, pair)
            o = attend(two, k, v, tile_bias)
            for j in (0, 1):
                of = kv_head * ratio + 2 * pair + j
                t = jnp.sum(jnp.where(gate_at == of, gates, 0.0), axis=1, keepdims=True)
                where = pl.ds(at + j * HEAD_SIZE, HEAD_SIZE)
                total = self_out[:, where] + (t * present) * o[j * rows : (j + 1) * rows]
                out[:, where] = total.astype(BF16)
        return 0

    lax.fori_loop(0, kv_heads, cross_head, 0)

    send_wo.wait_send()
    send_va.wait_send()
    if ring:
        for c in [*right_way.values(), *left_way.values(), *across]:
            c.wait_send()
    for d in (1, 2):
        @pl.when(s + d < n)
        def _():
            ids[d - 1].wait_send()

    @pl.when(s + 2 < n)
    def _():
        far.wait_send()

    @pl.when(has_close)
    def _():
        close.wait_send()

    @pl.when(has_back)
    def _():
        back.wait_send()

    @pl.when(s + 1 < n)
    def _():
        send_img.wait_send()

    @pl.when(s >= 1)
    def _():
        pass_img.wait_send()


def per_device(
    groups, n, text_query_rows, text_key_value, doc_ids, tile_span, vision_hidden, vision_qkv,
    vision_out_weight, cross_keyvalue_weight, cross_gate,
):
    rows, q_cols = text_query_rows.shape
    tile, width = vision_hidden.shape
    kv_cols = text_key_value.shape[2]
    part = vision_qkv.shape[2]
    shard = cross_keyvalue_weight.shape[0]
    ring = n == RING_PLACES and groups == 2 and shard % 160 == 0
    weight = cross_keyvalue_weight.reshape(shard, 2 * kv_cols)
    if not ring:
        weight = lax.all_gather(weight, "seq", axis=0, tiled=True)
    anywhere = pl.BlockSpec(memory_space=pl.ANY)
    vmem = pl.BlockSpec(memory_space=pltpu.VMEM)
    return pl.pallas_call(
        functools.partial(kernel, n, ring),
        out_shape=jax.ShapeDtypeStruct((rows, q_cols), BF16),
        in_specs=[anywhere, anywhere, vmem, vmem, anywhere, anywhere, anywhere, anywhere, vmem],
        out_specs=vmem,
        scratch_shapes=[
            pltpu.VMEM((rows, q_cols), BF16),
            pltpu.VMEM((2, 3 * rows, kv_cols), BF16),
            pltpu.VMEM((2, 1, rows), jnp.int32),
            pltpu.VMEM((tile, width), BF16),
            pltpu.VMEM((3, tile, part), BF16),
            pltpu.VMEM((2, part, width), BF16),
            pltpu.VMEM((width, 2 * kv_cols), BF16),
            pltpu.VMEM((2, tile, part), BF16),
            pltpu.VMEM((tile, width), F32),
            pltpu.VMEM((2 * tile, width), BF16),
            pltpu.VMEM((2 * tile, 2 * kv_cols), BF16),
            pltpu.VMEM((rows, q_cols), F32),
            pltpu.SemaphoreType.DMA((SEMS,)),
            pltpu.SemaphoreType.DMA((SEMS,)),
            pltpu.SemaphoreType.DMA((8,)),
        ],
        compiler_params=pltpu.CompilerParams(
            collective_id=0, has_side_effects=True, vmem_limit_bytes=62 * 1024 * 1024
        ),
    )(
        text_query_rows, text_key_value, doc_ids.reshape(1, rows), tile_span.T,
        vision_hidden, vision_qkv, vision_out_weight, weight,
        cross_gate.reshape(1, -1),
    )


def solution(mesh):
    placed = (
        P(("groups", "seq"), "head"),
        P(None, ("groups", "seq"), "head"),
        P(("groups", "seq")),
        P(("groups", "seq"), None),
        P(("groups", "seq"), None),
        P(None, ("groups", "seq"), "head"),
        P("head", None),
        P("seq", None, "head"),
        P("head"),
    )
    return jax.shard_map(
        functools.partial(per_device, mesh.shape["groups"], mesh.shape["seq"]),
        mesh=mesh,
        in_specs=placed,
        out_specs=P(("groups", "seq"), "head"),
        check_vma=False,
    )
```
